32 devices in a mesh: groups: 2 (over x), row: 16 (over z, y, core).
Axes of the slice: x: 2, y: 2, z: 4, core: 2. Of those that a mesh axis runs over, the one named last changes fastest.
Arguments:
- base_grid: float32 [8192, 2048], P(('groups', 'row')), parts along dimension 0, may hold values from -6 to 6
- strip_minima: float32 [4096, 8, 128], P(('groups', 'row')), parts along dimension 0, may hold values from -6 to 6
- strip_owner: int32 [4096, 1], P(('groups', 'row')), parts along dimension 0, may hold values from 0 to 15; in each aligned block of 128 rows (0 to 127, 128 to 255, ...) at most 16 rows name the same one
- strip_cell: int32 [4096], P(('groups', 'row')), parts along dimension 0, may hold values from 0 to 511
Outputs:
- merged: float32 [8192, 2048], P(('groups', 'row')), parts along dimension 0
- opened_first: float32 [8192, 2048], P(('groups', 'row')), parts along dimension 0
- ground: float32 [8192, 2048], P(('groups', 'row')), parts along dimension 0
The draws below stay inside these ranges and needn't reach their ends.
There are 2 independent parts, one for each index of `groups`. The reference program is written for one: setup_inputs(seed, part) draws one part's arguments, and reference() takes and returns one part's arrays. A program takes and returns all parts, laid end to end along the dimension named above; each array names one. Nothing has to cross between parts.
Inputs may be any that keep to these rules, and one draw needn't show every extreme that they name: `strip_owner`: among the strip blocks of one device no owner is named more than 16 times, a bound that some block reaches.
All inputs are finite; a program needn't handle non-finite values.
Results may differ from the reference program's by a relative error of at most 0.00002.
Values sent between devices are 32-bit elements; how exact they have to be, the bound alone decides.
A program may use at most 64 MiB of HBM per device.

```python
import math
import jax
import jax.numpy as jnp
import numpy as np
from jax import lax

ROWS = 256
COLS = 2048
SB_DEV = 128
BR = 8
BC = 128
HALF1 = 32
HALF2 = 64
NR = 4096
BLK_DEV = 512
CAP = 16
N_ROW = 16


def touch_ends(entries, own_key, smallest, largest):
    place = [jax.random.randint(jax.random.fold_in(own_key, axis), (), 0, length) for axis, length in enumerate(entries.shape)]
    main_axis = entries.shape.index(max(entries.shape))
    beside = place[:main_axis] + [(place[main_axis] + 1) % entries.shape[main_axis]] + place[main_axis + 1:]
    return entries.at[tuple(place)].set(smallest).at[tuple(beside)].set(largest)


def block_levels(rng, extent, cuts, least, high):
    def one(axis_at, parts):
        draws = jax.random.uniform(jax.random.fold_in(jax.random.fold_in(rng, 6), axis_at), (parts,), jnp.float32, least / len(cuts), high / len(cuts))
        return jnp.repeat(jnp.exp(draws), extent[axis_at] // parts).reshape((-1,) + (1,) * (len(extent) - axis_at - 1))

    loudness = one(*cuts[0])
    for cut in cuts[1:]:
        loudness = loudness * one(*cut)
    return loudness


def assign_block(own_key, own, number, rows, number_of, top, bound, lean):
    ranking = jax.random.permutation(own_key, number_of)
    heavy_load, common = shares(number_of, rows * top, bound, lean, True), shares(number_of, rows * top, bound, lean, False)
    places = jnp.arange(number_of)

    def named(sizes, rotation):
        used = int((sizes > 0).sum())
        fixed = max(1, used // 4)
        shifted = fixed + (places - fixed + rotation * (used - fixed)) % max(1, number_of - fixed)
        return jnp.zeros((number_of,), jnp.int32).at[ranking[jnp.where(places < fixed, places, shifted)]].set(jnp.asarray(sizes, jnp.int32))

    sizes = jnp.where(number % 4 == 0, named(heavy_load, number // 4), named(common, number - number // 4 - 1))
    mixed = jax.random.permutation(jax.random.fold_in(own, 3), number_of)
    donor, receiver = mixed[0:number_of // 2 * 2:2], mixed[1:number_of // 2 * 2:2]
    room = jnp.minimum(sizes[donor] - 1, bound - sizes[receiver]) // 2
    room = jnp.where((donor == ranking[0]) | (receiver == ranking[0]) | (sizes[receiver] == 0), 0, jnp.maximum(room, 0))
    shifted = jax.random.randint(jax.random.fold_in(own, 4), (number_of // 2,), 0, 1 << 20) % (room + 1)
    sizes = sizes.at[donor].add(-shifted).at[receiver].add(shifted)
    members = jnp.searchsorted(jnp.cumsum(sizes), jnp.arange(rows * top), side="right").astype(jnp.int32)
    table = members.reshape(top, rows).T
    table = table[jax.random.permutation(jax.random.fold_in(own, 1), rows)]
    rotation = jax.random.randint(jax.random.fold_in(own, 2), (rows, 1), 0, top)
    return jnp.take_along_axis(table, (jnp.arange(top)[None, :] + rotation) % top, axis=1)


def shares(count, total, reach, lean, full):
    weights = [(1 << 20) // math.isqrt(rank ** lean) + 1 for rank in range(1, count + 1)]
    largest = reach if full else min(reach, max(-(-total // count), total * weights[0] // sum(weights)))
    least = 1 if total - largest >= count - 1 else 0
    holding, surplus = [largest] + [least] * (count - 1), total - largest - least * (count - 1)
    while surplus > 0:
        free = [i for i in range(1, count) if holding[i] < largest] or [i for i in range(1, count) if holding[i] < reach]
        mass, remaining = sum([weights[i] for i in free]), surplus
        for i in free:
            more = min(reach - holding[i], max(1, remaining * weights[i] // mass), surplus)
            holding[i] = holding[i] + more
            surplus = surplus - more
    return np.array(holding)


def bell_draw(rng, extent, width, limit, cuts=(), dtype=jnp.bfloat16):
    factor_of = block_levels(rng, extent, cuts, -0.22, 0.18) if cuts else 1.0
    result = jax.random.normal(rng, extent, jnp.float32) * width * factor_of
    return jnp.minimum(jnp.maximum(result, -limit), limit).astype(dtype)


def setup_inputs(seed: int = 0, part: int = 0) -> dict:
    key_of = jax.random.split(jax.random.key(seed), 5)
    part_keys = jax.random.split(jax.random.fold_in(key_of[4], part), 5)
    base_grid = bell_draw(part_keys[0], (NR, COLS), 1.0, 6.0, ((0, 16),), jnp.float32)
    strip_minima = bell_draw(part_keys[1], (N_ROW * SB_DEV, BR, BC), 1.0, 6.0, ((0, 16),), jnp.float32)
    strip_owner_keys = jax.random.split(jax.random.fold_in(part_keys[2], 1), (N_ROW * SB_DEV) // SB_DEV)
    strip_owner_turns = jax.random.permutation(jax.random.fold_in(part_keys[2], 3), (N_ROW * SB_DEV) // SB_DEV)
    strip_owner = jax.vmap(lambda own, number: assign_block(jax.random.fold_in(part_keys[2], 2), own, number, SB_DEV, N_ROW, 1, CAP, 2))(strip_owner_keys, strip_owner_turns).reshape((N_ROW * SB_DEV, 1))
    strip_cell = touch_ends(jax.random.randint(part_keys[3], (N_ROW * SB_DEV,), 0, BLK_DEV), jax.random.fold_in(part_keys[3], 1), 0, BLK_DEV - 1).astype(jnp.int32)
    return {"base_grid": base_grid, "strip_minima": strip_minima, "strip_owner": strip_owner, "strip_cell": strip_cell}


def slide(values, half, axis, take_min):
    combine = jnp.minimum if take_min else jnp.maximum
    length = 2 * half + 1
    span = 1
    running = values
    while 2 * span <= length:
        size = running.shape[axis]
        running = combine(lax.slice_in_dim(running, 0, size - span, axis=axis), lax.slice_in_dim(running, span, size, axis=axis))
        span = span * 2
    count = values.shape[axis] - length + 1
    return combine(lax.slice_in_dim(running, 0, count, axis=axis), lax.slice_in_dim(running, length - span, length - span + count, axis=axis))


def square(values, half, take_min):
    fill = jnp.inf if take_min else -jnp.inf
    padded = jnp.pad(values, ((half, half), (half, half)), constant_values=fill)
    return slide(slide(padded, half, 0, take_min), half, 1, take_min)


def opening(values, half):
    return square(square(values, half, True), half, False)


def reference(base_grid, strip_minima, strip_owner, strip_cell):
    band_blocks = ROWS // BR
    col_blocks = COLS // BC
    grid = base_grid.reshape(N_ROW, band_blocks, BR, col_blocks, BC)
    owner = strip_owner[:, 0].astype(jnp.int32)
    block_row = (strip_cell // col_blocks).astype(jnp.int32)
    block_col = (strip_cell % col_blocks).astype(jnp.int32)
    grid = grid.at[owner, block_row, :, block_col, :].min(strip_minima)
    merged = grid.reshape(base_grid.shape)
    opened_first = opening(merged, HALF1)
    ground = opening(opened_first, HALF2)
    return merged, opened_first, ground
```

```python
import functools

import jax
import jax.numpy as jnp
from jax import lax
from jax.experimental import pallas as pl
from jax.experimental.pallas import tpu as pltpu
from jax.sharding import PartitionSpec as P

BR = 8
BC = 128
HALF1 = 32
HALF2 = 64
MESH = pl.DeviceIdType.MESH
VMEM_LIMIT = 48 * 1024 * 1024


def pack_kernel(count, capacity, held, owner_ref, cell_ref, strips_ref, box_ref, used_ref):
    lane = lax.broadcasted_iota(jnp.int32, (1, BC), 1)

    def clear(i, c):
        used_ref[i] = 0
        box_ref[i, capacity] = jnp.full((BR, BC), -1.0, jnp.float32)
        return c

    lax.fori_loop(0, count, clear, 0)

    def place(k, c):
        owner = owner_ref[k]
        slot = used_ref[owner]
        used_ref[owner] = slot + 1
        box_ref[owner, slot] = strips_ref[k]
        tags = box_ref[owner, capacity, 0:1, :]
        box_ref[owner, capacity, 0:1, :] = jnp.where(
            lane == slot, cell_ref[k].astype(jnp.float32), tags
        )
        return c

    lax.fori_loop(0, held, place, 0)


def merge_kernel(entries, capacity, col_blocks, tags_ref, base_ref, box_ref, out_ref):
    out_ref[...] = base_ref[...]

    def place(e, c):
        tag = tags_ref[e]

        @pl.when(tag >= 0)
        def _():
            row = pl.multiple_of((tag // col_blocks) * BR, BR)
            col = pl.multiple_of((tag % col_blocks) * BC, BC)
            here = (pl.ds(row, BR), pl.ds(col, BC))
            out_ref[here] = jnp.minimum(out_ref[here], box_ref[e // capacity, e % capacity])

        return c

    lax.fori_loop(0, entries, place, 0)


def across(x, half, take_min):
    combine = jnp.minimum if take_min else jnp.maximum
    fill = jnp.inf if take_min else -jnp.inf
    cols = x.shape[1]
    run = jnp.concatenate([x, jnp.full((x.shape[0], BC), fill, jnp.float32)], axis=1)
    width = cols + BC
    span = 1
    while span < half:
        run = combine(run, pltpu.roll(run, width - span, axis=1))
        span *= 2
    run = combine(run, pltpu.roll(run, half, axis=1))
    run = combine(run, pltpu.roll(run, width - 1, axis=1))
    return run[:, :cols]


def down(x, half, take_min):
    combine = jnp.minimum if take_min else jnp.maximum
    rows = x.shape[0]
    run = x
    span = 1
    while span < 8:
        run = combine(run, pltpu.roll(run, rows - span, axis=0))
        span *= 2
    while span < 2 * half:
        size = run.shape[0]
        run = combine(run[: size - span], run[span:])
        span *= 2
    keep = rows - 2 * half
    return combine(run[:keep], x[2 * half :])


def open_rows(src, first, out, dst, dst_first, half, is_top, is_bottom):
    def body(c, carry):
        cols = pl.ds(pl.multiple_of(c * BC, BC), BC)
        low = down(src[first : first + out + 4 * half, cols], half, True)
        parts = [low[:half], low[half : half + out], low[half + out :]]
        if is_top is not None:
            parts[0] = jnp.where(is_top, -jnp.inf, parts[0])
        if is_bottom is not None:
            parts[2] = jnp.where(is_bottom, -jnp.inf, parts[2])
        dst[dst_first : dst_first + out, cols] = down(jnp.concatenate(parts, axis=0), half, False)
        return carry

    lax.fori_loop(0, src.shape[1] // BC, body, 0)


def row_blocks(first, rows, body):
    def step(i, c):
        body(pl.multiple_of(first + i * 8, 8))
        return c

    lax.fori_loop(0, rows // 8, step, 0)


def open_kernel(n, m_ref, first_ref, ground_ref, near, far, mid, send_sem, recv_sem):
    place = lax.axis_index("row")
    rows = m_ref.shape[0]
    is_top, is_bottom = place == 0, place == n - 1
    edge1, edge2 = 2 * HALF1, 2 * HALF2

    barrier = pltpu.get_barrier_semaphore()

    @pl.when(place > 0)
    def _():
        pl.semaphore_signal(barrier, inc=1, device_id={"row": place - 1}, device_id_type=MESH)

    @pl.when(place < n - 1)
    def _():
        pl.semaphore_signal(barrier, inc=1, device_id={"row": place + 1}, device_id_type=MESH)

    pl.semaphore_wait(barrier, jnp.where(is_top | is_bottom, 1, 2))

    def up(buf, src, dst, size, at):
        return pltpu.make_async_remote_copy(
            src_ref=buf.at[pl.ds(src, size)],
            dst_ref=buf.at[pl.ds(dst, size)],
            send_sem=send_sem.at[at],
            recv_sem=recv_sem.at[at],
            device_id={"row": place - 1},
            device_id_type=MESH,
        )

    def down_to(buf, src, dst, size, at):
        return pltpu.make_async_remote_copy(
            src_ref=buf.at[pl.ds(src, size)],
            dst_ref=buf.at[pl.ds(dst, size)],
            send_sem=send_sem.at[at],
            recv_sem=recv_sem.at[at],
            device_id={"row": place + 1},
            device_id_type=MESH,
        )

    plans = [
        (near, (edge1, edge1 + rows, edge1), (rows, 0, edge1)),
        (far, (edge2 + 64, edge2 + rows + 64, 64), (edge2 + 128, 0, 64)),
        (far, (edge2, edge2 + rows, 64), (edge2 + 192, 64, 64)),
    ]

    def start(i):
        buf, u, d = plans[i]

        @pl.when(place > 0)
        def _():
            up(buf, *u, 2 * i).start()

        @pl.when(place < n - 1)
        def _():
            down_to(buf, *d, 2 * i + 1).start()

    def receive(i):
        buf, u, d = plans[i]

        @pl.when(place < n - 1)
        def _():
            up(buf, *u, 2 * i).wait_recv()

        @pl.when(place > 0)
        def _():
            down_to(buf, *d, 2 * i + 1).wait_recv()

    def sent(i):
        buf, u, d = plans[i]

        @pl.when(place > 0)
        def _():
            up(buf, *u, 2 * i).wait_send()

        @pl.when(place < n - 1)
        def _():
            down_to(buf, *d, 2 * i + 1).wait_send()

    def narrow(r):
        near[pl.ds(r + edge1, 8), :] = across(m_ref[pl.ds(r, 8), :], HALF1, True)

    def finish_first(r):
        y = across(mid[pl.ds(r, 8), :], HALF1, False)
        first_ref[pl.ds(r, 8), :] = y
        far[pl.ds(r + edge2, 8), :] = across(y, HALF2, True)

    row_blocks(0, 64, narrow)
    row_blocks(rows - 64, 64, narrow)
    start(0)

    @pl.when(is_top)
    def _():
        near[0:edge1, :] = jnp.full((edge1, near.shape[1]), jnp.inf, jnp.float32)
        far[0:edge2, :] = jnp.full((edge2, far.shape[1]), jnp.inf, jnp.float32)

    @pl.when(is_bottom)
    def _():
        near[edge1 + rows :, :] = jnp.full((edge1, near.shape[1]), jnp.inf, jnp.float32)
        far[edge2 + rows :, :] = jnp.full((edge2, far.shape[1]), jnp.inf, jnp.float32)

    row_blocks(64, rows - 128, narrow)
    open_rows(near, edge1, rows - 128, mid, 64, HALF1, None, None)
    row_blocks(64, rows - 128, finish_first)
    start(1)
    receive(0)
    open_rows(near, 0, 64, mid, 0, HALF1, is_top, None)
    open_rows(near, rows - 64, 64, mid, rows - 64, HALF1, None, is_bottom)
    row_blocks(0, 64, finish_first)
    row_blocks(rows - 64, 64, finish_first)
    start(2)
    receive(1)
    receive(2)
    open_rows(far, 0, rows, mid, 0, HALF2, is_top, is_bottom)

    def finish_ground(r):
        ground_ref[pl.ds(r, 8), :] = across(mid[pl.ds(r, 8), :], HALF2, False)

    row_blocks(0, rows, finish_ground)
    for i in range(3):
        sent(i)


def on_device(n, base_grid, strip_minima, strip_owner, strip_cell):
    held = strip_minima.shape[0]
    capacity = max(2, 2 * held // n)
    rows, cols = base_grid.shape
    vmem = pl.BlockSpec(memory_space=pltpu.VMEM)
    smem = pl.BlockSpec(memory_space=pltpu.SMEM)
    outbox = pl.pallas_call(
        functools.partial(pack_kernel, n, capacity, held),
        out_shape=jax.ShapeDtypeStruct((n, capacity + 1, BR, BC), jnp.float32),
        in_specs=[smem, smem, vmem],
        out_specs=vmem,
        scratch_shapes=[pltpu.SMEM((n,), jnp.int32)],
        compiler_params=pltpu.CompilerParams(vmem_limit_bytes=VMEM_LIMIT),
        name="pack",
    )(strip_owner[:, 0], strip_cell, strip_minima)
    inbox = lax.all_to_all(outbox, "row", split_axis=0, concat_axis=0, tiled=True)
    tags = inbox[:, capacity, 0, :capacity].astype(jnp.int32).reshape(-1)
    merged = pl.pallas_call(
        functools.partial(merge_kernel, n * capacity, capacity, cols // BC),
        out_shape=jax.ShapeDtypeStruct((rows, cols), jnp.float32),
        in_specs=[smem, vmem, vmem],
        out_specs=vmem,
        compiler_params=pltpu.CompilerParams(vmem_limit_bytes=VMEM_LIMIT),
        name="merge",
    )(tags, base_grid, inbox)
    shape = jax.ShapeDtypeStruct((rows, cols), jnp.float32)
    opened_first, ground = pl.pallas_call(
        functools.partial(open_kernel, n),
        out_shape=(shape, shape),
        in_specs=[vmem],
        out_specs=(vmem, vmem),
        scratch_shapes=[
            pltpu.VMEM((rows + 4 * HALF1, cols), jnp.float32),
            pltpu.VMEM((rows + 4 * HALF2, cols), jnp.float32),
            pltpu.VMEM((rows, cols), jnp.float32),
            pltpu.SemaphoreType.DMA((6,)),
            pltpu.SemaphoreType.DMA((6,)),
        ],
        compiler_params=pltpu.CompilerParams(
            collective_id=0, has_side_effects=True, vmem_limit_bytes=VMEM_LIMIT
        ),
        name="opening",
    )(merged)
    return (merged, opened_first, ground)


def solution(mesh):
    in_specs = (
        P(("groups", "row"), None),
        P(("groups", "row"), None, None),
        P(("groups", "row"), None),
        P(("groups", "row")),
    )
    out_specs = (P(("groups", "row"), None), P(("groups", "row"), None), P(("groups", "row"), None))
    return jax.shard_map(
        functools.partial(on_device, mesh.shape["row"]),
        mesh=mesh,
        in_specs=in_specs,
        out_specs=out_specs,
        check_vma=False,
    )
```

```python
import functools

import jax
import jax.numpy as jnp
from jax import lax
from jax.experimental import pallas as pl
from jax.experimental.pallas import tpu as pltpu
from jax.sharding import PartitionSpec as P

BR = 8
BC = 128
HALF1 = 32
HALF2 = 64
TALL = 64
MESH = pl.DeviceIdType.MESH
VMEM_LIMIT = 48 * 1024 * 1024


def pack_kernel(count, capacity, held, owner_ref, cell_ref, strips_ref, box_ref, used_ref):
    lane = lax.broadcasted_iota(jnp.int32, (1, BC), 1)

    def clear(i, c):
        used_ref[i] = 0
        box_ref[i, capacity] = jnp.full((BR, BC), -1.0, jnp.float32)
        return c

    lax.fori_loop(0, count, clear, 0)

    def place(k, c):
        owner = owner_ref[k]
        slot = used_ref[owner]
        used_ref[owner] = slot + 1
        box_ref[owner, slot] = strips_ref[k]
        tags = box_ref[owner, capacity, 0:1, :]
        box_ref[owner, capacity, 0:1, :] = jnp.where(
            lane == slot, cell_ref[k].astype(jnp.float32), tags
        )
        return c

    lax.fori_loop(0, held, place, 0)


def merge_kernel(entries, capacity, col_blocks, tags_ref, base_ref, box_ref, out_ref):
    out_ref[...] = base_ref[...]

    def place(e, c):
        tag = tags_ref[e]

        @pl.when(tag >= 0)
        def _():
            row = pl.multiple_of((tag // col_blocks) * BR, BR)
            col = pl.multiple_of((tag % col_blocks) * BC, BC)
            here = (pl.ds(row, BR), pl.ds(col, BC))
            out_ref[here] = jnp.minimum(out_ref[here], box_ref[e // capacity, e % capacity])

        return c

    lax.fori_loop(0, entries, place, 0)


def across(x, half, take_min):
    combine = jnp.minimum if take_min else jnp.maximum
    fill = jnp.inf if take_min else -jnp.inf
    cols = x.shape[1]
    run = jnp.concatenate([x, jnp.full((x.shape[0], BC), fill, jnp.float32)], axis=1)
    width = cols + BC
    span = 1
    while span < half:
        run = combine(run, pltpu.roll(run, width - span, axis=1))
        span *= 2
    run = combine(run, pltpu.roll(run, half, axis=1))
    run = combine(run, pltpu.roll(run, width - 1, axis=1))
    return run[:, :cols]


def down(x, half, take_min):
    combine = jnp.minimum if take_min else jnp.maximum
    rows = x.shape[0]
    run = x
    span = 1
    while span < 8:
        run = combine(run, pltpu.roll(run, rows - span, axis=0))
        span *= 2
    while span < 2 * half:
        size = run.shape[0]
        run = combine(run[: size - span], run[span:])
        span *= 2
    keep = rows - 2 * half
    return combine(run[:keep], x[2 * half :])


def open_rows(src, first, out, dst, dst_first, half, is_top, is_bottom):
    def body(c, carry):
        cols = pl.ds(pl.multiple_of(c * BC, BC), BC)
        low = down(src[first : first + out + 4 * half, cols], half, True)
        parts = [low[:half], low[half : half + out], low[half + out :]]
        if is_top is not None:
            parts[0] = jnp.where(is_top, -jnp.inf, parts[0])
        if is_bottom is not None:
            parts[2] = jnp.where(is_bottom, -jnp.inf, parts[2])
        dst[dst_first : dst_first + out, cols] = down(jnp.concatenate(parts, axis=0), half, False)
        return carry

    lax.fori_loop(0, src.shape[1] // BC, body, 0)


def row_blocks(first, rows, body):
    def step(i, c):
        body(pl.multiple_of(first + i * TALL, TALL))
        return c

    lax.fori_loop(0, rows // TALL, step, 0)


def open_kernel(n, m_ref, first_ref, ground_ref, near, far, mid, send_sem, recv_sem):
    place = lax.axis_index("row")
    rows = m_ref.shape[0]
    is_top, is_bottom = place == 0, place == n - 1
    edge1, edge2 = 2 * HALF1, 2 * HALF2

    barrier = pltpu.get_barrier_semaphore()

    @pl.when(place > 0)
    def _():
        pl.semaphore_signal(barrier, inc=1, device_id={"row": place - 1}, device_id_type=MESH)

    @pl.when(place < n - 1)
    def _():
        pl.semaphore_signal(barrier, inc=1, device_id={"row": place + 1}, device_id_type=MESH)

    pl.semaphore_wait(barrier, jnp.where(is_top | is_bottom, 1, 2))

    def up(buf, src, dst, size, at):
        return pltpu.make_async_remote_copy(
            src_ref=buf.at[pl.ds(src, size)],
            dst_ref=buf.at[pl.ds(dst, size)],
            send_sem=send_sem.at[at],
            recv_sem=recv_sem.at[at],
            device_id={"row": place - 1},
            device_id_type=MESH,
        )

    def down_to(buf, src, dst, size, at):
        return pltpu.make_async_remote_copy(
            src_ref=buf.at[pl.ds(src, size)],
            dst_ref=buf.at[pl.ds(dst, size)],
            send_sem=send_sem.at[at],
            recv_sem=recv_sem.at[at],
            device_id={"row": place + 1},
            device_id_type=MESH,
        )

    plans = [
        (near, (edge1, edge1 + rows, edge1), (rows, 0, edge1)),
        (far, (edge2 + 64, edge2 + rows + 64, 64), (edge2 + 128, 0, 64)),
        (far, (edge2, edge2 + rows, 64), (edge2 + 192, 64, 64)),
    ]

    def start(i):
        buf, u, d = plans[i]

        @pl.when(place > 0)
        def _():
            up(buf, *u, 2 * i).start()

        @pl.when(place < n - 1)
        def _():
            down_to(buf, *d, 2 * i + 1).start()

    def receive(i):
        buf, u, d = plans[i]

        @pl.when(place < n - 1)
        def _():
            up(buf, *u, 2 * i).wait_recv()

        @pl.when(place > 0)
        def _():
            down_to(buf, *d, 2 * i + 1).wait_recv()

    def sent(i):
        buf, u, d = plans[i]

        @pl.when(place > 0)
        def _():
            up(buf, *u, 2 * i).wait_send()

        @pl.when(place < n - 1)
        def _():
            down_to(buf, *d, 2 * i + 1).wait_send()

    def narrow(r):
        near[pl.ds(r + edge1, TALL), :] = across(m_ref[pl.ds(r, TALL), :], HALF1, True)

    def finish_first(r):
        y = across(mid[pl.ds(r, TALL), :], HALF1, False)
        first_ref[pl.ds(r, TALL), :] = y
        far[pl.ds(r + edge2, TALL), :] = across(y, HALF2, True)

    row_blocks(0, 64, narrow)
    row_blocks(rows - 64, 64, narrow)
    start(0)

    @pl.when(is_top)
    def _():
        near[0:edge1, :] = jnp.full((edge1, near.shape[1]), jnp.inf, jnp.float32)
        far[0:edge2, :] = jnp.full((edge2, far.shape[1]), jnp.inf, jnp.float32)

    @pl.when(is_bottom)
    def _():
        near[edge1 + rows :, :] = jnp.full((edge1, near.shape[1]), jnp.inf, jnp.float32)
        far[edge2 + rows :, :] = jnp.full((edge2, far.shape[1]), jnp.inf, jnp.float32)

    row_blocks(64, rows - 128, narrow)
    open_rows(near, edge1, rows - 128, mid, 64, HALF1, None, None)
    row_blocks(64, rows - 128, finish_first)
    start(1)
    receive(0)
    open_rows(near, 0, 64, mid, 0, HALF1, is_top, None)
    open_rows(near, rows - 64, 64, mid, rows - 64, HALF1, None, is_bottom)
    row_blocks(0, 64, finish_first)
    row_blocks(rows - 64, 64, finish_first)
    start(2)
    receive(1)
    receive(2)
    open_rows(far, 0, rows, mid, 0, HALF2, is_top, is_bottom)

    def finish_ground(r):
        ground_ref[pl.ds(r, TALL), :] = across(mid[pl.ds(r, TALL), :], HALF2, False)

    row_blocks(0, rows, finish_ground)
    for i in range(3):
        sent(i)


def on_device(n, base_grid, strip_minima, strip_owner, strip_cell):
    held = strip_minima.shape[0]
    capacity = max(2, 2 * held // n)
    rows, cols = base_grid.shape
    vmem = pl.BlockSpec(memory_space=pltpu.VMEM)
    smem = pl.BlockSpec(memory_space=pltpu.SMEM)
    outbox = pl.pallas_call(
        functools.partial(pack_kernel, n, capacity, held),
        out_shape=jax.ShapeDtypeStruct((n, capacity + 1, BR, BC), jnp.float32),
        in_specs=[smem, smem, vmem],
        out_specs=vmem,
        scratch_shapes=[pltpu.SMEM((n,), jnp.int32)],
        compiler_params=pltpu.CompilerParams(vmem_limit_bytes=VMEM_LIMIT),
        name="pack",
    )(strip_owner[:, 0], strip_cell, strip_minima)
    inbox = lax.all_to_all(outbox, "row", split_axis=0, concat_axis=0, tiled=True)
    tags = inbox[:, capacity, 0, :capacity].astype(jnp.int32).reshape(-1)
    merged = pl.pallas_call(
        functools.partial(merge_kernel, n * capacity, capacity, cols // BC),
        out_shape=jax.ShapeDtypeStruct((rows, cols), jnp.float32),
        in_specs=[smem, vmem, vmem],
        out_specs=vmem,
        compiler_params=pltpu.CompilerParams(vmem_limit_bytes=VMEM_LIMIT),
        name="merge",
    )(tags, base_grid, inbox)
    shape = jax.ShapeDtypeStruct((rows, cols), jnp.float32)
    opened_first, ground = pl.pallas_call(
        functools.partial(open_kernel, n),
        out_shape=(shape, shape),
        in_specs=[vmem],
        out_specs=(vmem, vmem),
        scratch_shapes=[
            pltpu.VMEM((rows + 4 * HALF1, cols), jnp.float32),
            pltpu.VMEM((rows + 4 * HALF2, cols), jnp.float32),
            pltpu.VMEM((rows, cols), jnp.float32),
            pltpu.SemaphoreType.DMA((6,)),
            pltpu.SemaphoreType.DMA((6,)),
        ],
        compiler_params=pltpu.CompilerParams(
            collective_id=0, has_side_effects=True, vmem_limit_bytes=VMEM_LIMIT
        ),
        name="opening",
    )(merged)
    return (merged, opened_first, ground)


def solution(mesh):
    in_specs = (
        P(("groups", "row"), None),
        P(("groups", "row"), None, None),
        P(("groups", "row"), None),
        P(("groups", "row")),
    )
    out_specs = (P(("groups", "row"), None), P(("groups", "row"), None), P(("groups", "row"), None))
    return jax.shard_map(
        functools.partial(on_device, mesh.shape["row"]),
        mesh=mesh,
        in_specs=in_specs,
        out_specs=out_specs,
        check_vma=False,
    )
```

```python
import functools

import jax
import jax.numpy as jnp
from jax import lax
from jax.experimental import pallas as pl
from jax.experimental.pallas import tpu as pltpu
from jax.sharding import PartitionSpec as P

BR = 8
BC = 128
HALF1 = 32
HALF2 = 64
TALL = 64
PIECES = 4
MESH = pl.DeviceIdType.MESH
VMEM_LIMIT = 48 * 1024 * 1024


def pack_kernel(count, capacity, held, owner_ref, cell_ref, strips_ref, box_ref, used_ref):
    lane = lax.broadcasted_iota(jnp.int32, (1, BC), 1)

    def clear(i, c):
        used_ref[i] = 0
        box_ref[i, capacity] = jnp.full((BR, BC), -1.0, jnp.float32)
        return c

    lax.fori_loop(0, count, clear, 0)

    def place(k, c):
        owner = owner_ref[k]
        slot = used_ref[owner]
        used_ref[owner] = slot + 1
        box_ref[owner, slot] = strips_ref[k]
        tags = box_ref[owner, capacity, 0:1, :]
        box_ref[owner, capacity, 0:1, :] = jnp.where(
            lane == slot, cell_ref[k].astype(jnp.float32), tags
        )
        return c

    lax.fori_loop(0, held, place, 0)


def exchange_kernel(n, box_ref, in_ref, send_sem, recv_sem, own_sem):
    me = lax.axis_index("row")
    barrier = pltpu.get_barrier_semaphore()

    def greet(k, c):
        peer = lax.rem(me + k, n)
        pl.semaphore_signal(barrier, inc=1, device_id={"row": peer}, device_id_type=MESH)
        return c

    lax.fori_loop(1, n, greet, 0)
    own = pltpu.make_async_copy(box_ref.at[me], in_ref.at[me], own_sem)
    own.start()
    pl.semaphore_wait(barrier, n - 1)

    def copy(peer, slot):
        return pltpu.make_async_remote_copy(
            src_ref=box_ref.at[peer],
            dst_ref=in_ref.at[slot],
            send_sem=send_sem.at[peer],
            recv_sem=recv_sem.at[slot],
            device_id={"row": peer},
            device_id_type=MESH,
        )

    def send(k, c):
        copy(lax.rem(me + k, n), me).start()
        return c

    lax.fori_loop(1, n, send, 0)

    def finish(k, c):
        peer = lax.rem(me + k, n)
        copy(peer, peer).wait_recv()
        copy(peer, me).wait_send()
        return c

    lax.fori_loop(1, n, finish, 0)
    own.wait()


def merge_kernel(n, capacity, col_blocks, tags_ref, base_ref, box_ref, out_ref):
    out_ref[...] = base_ref[...]
    bits = col_blocks.bit_length() - 1

    def place(s, c):
        for j in range(capacity):
            tag = tags_ref[s * capacity + j]
            cell = jnp.maximum(tag, 0)
            row = pl.multiple_of((cell >> bits) * BR, BR)
            col = pl.multiple_of((cell & (col_blocks - 1)) * BC, BC)
            here = (pl.ds(row, BR), pl.ds(col, BC))
            block = jnp.where(tag >= 0, box_ref[s, j], jnp.inf)
            out_ref[here] = jnp.minimum(out_ref[here], block)
        return c

    lax.fori_loop(0, n, place, 0)


def across(x, half, take_min):
    combine = jnp.minimum if take_min else jnp.maximum
    fill = jnp.inf if take_min else -jnp.inf
    cols = x.shape[1]
    run = jnp.concatenate([x, jnp.full((x.shape[0], BC), fill, jnp.float32)], axis=1)
    width = cols + BC
    span = 1
    while span < half:
        run = combine(run, pltpu.roll(run, width - span, axis=1))
        span *= 2
    run = combine(run, pltpu.roll(run, half, axis=1))
    run = combine(run, pltpu.roll(run, width - 1, axis=1))
    return run[:, :cols]


def down(x, half, take_min):
    combine = jnp.minimum if take_min else jnp.maximum
    rows = x.shape[0]
    run = x
    span = 1
    while span < 8:
        run = combine(run, pltpu.roll(run, rows - span, axis=0))
        span *= 2
    while span < 2 * half:
        size = run.shape[0]
        run = combine(run[: size - span], run[span:])
        span *= 2
    keep = rows - 2 * half
    return combine(run[:keep], x[2 * half :])


def open_rows(src, first, out, dst, dst_first, half, is_top, is_bottom, start=0, stop=None):
    def body(c, carry):
        cols = pl.ds(pl.multiple_of(c * BC, BC), BC)
        low = down(src[first : first + out + 4 * half, cols], half, True)
        parts = [low[:half], low[half : half + out], low[half + out :]]
        if is_top is not None:
            parts[0] = jnp.where(is_top, -jnp.inf, parts[0])
        if is_bottom is not None:
            parts[2] = jnp.where(is_bottom, -jnp.inf, parts[2])
        dst[dst_first : dst_first + out, cols] = down(jnp.concatenate(parts, axis=0), half, False)
        return carry

    lax.fori_loop(start, src.shape[1] // BC if stop is None else stop, body, 0)


def row_blocks(first, rows, body):
    def step(i, c):
        body(pl.multiple_of(first + i * TALL, TALL))
        return c

    lax.fori_loop(0, rows // TALL, step, 0)


def open_kernel(n, m_ref, first_ref, ground_ref, near, far, mid, send_sem, recv_sem):
    place = lax.axis_index("row")
    rows = m_ref.shape[0]
    is_top, is_bottom = place == 0, place == n - 1
    edge1, edge2 = 2 * HALF1, 2 * HALF2
    width = m_ref.shape[1] // PIECES

    barrier = pltpu.get_barrier_semaphore()

    @pl.when(place > 0)
    def _():
        pl.semaphore_signal(barrier, inc=1, device_id={"row": place - 1}, device_id_type=MESH)

    @pl.when(place < n - 1)
    def _():
        pl.semaphore_signal(barrier, inc=1, device_id={"row": place + 1}, device_id_type=MESH)

    pl.semaphore_wait(barrier, jnp.where(is_top | is_bottom, 1, 2))

    def move(buf, src, dst, size, cols, peer, at):
        return pltpu.make_async_remote_copy(
            src_ref=buf.at[pl.ds(src, size), cols],
            dst_ref=buf.at[pl.ds(dst, size), cols],
            send_sem=send_sem.at[at],
            recv_sem=recv_sem.at[at],
            device_id={"row": peer},
            device_id_type=MESH,
        )

    plans = [
        (near, (edge1, edge1 + rows, edge1), (rows, 0, edge1), pl.ds(0, m_ref.shape[1])),
        (far, (edge2 + 64, edge2 + rows + 64, 64), (edge2 + 128, 0, 64), pl.ds(0, m_ref.shape[1])),
    ] + [
        (far, (edge2, edge2 + rows, 64), (edge2 + 192, 64, 64), pl.ds(c * width, width))
        for c in range(PIECES)
    ]

    def upward(i):
        return move(plans[i][0], *plans[i][1], plans[i][3], place - 1, 2 * i)

    def downward(i):
        return move(plans[i][0], *plans[i][2], plans[i][3], place + 1, 2 * i + 1)

    def start_up(*which):
        @pl.when(place > 0)
        def _():
            for i in which:
                upward(i).start()

    def start_down(*which):
        @pl.when(place < n - 1)
        def _():
            for i in which:
                downward(i).start()

    def receive(i):
        @pl.when(place < n - 1)
        def _():
            upward(i).wait_recv()

        @pl.when(place > 0)
        def _():
            downward(i).wait_recv()

    def sent(i):
        @pl.when(place > 0)
        def _():
            upward(i).wait_send()

        @pl.when(place < n - 1)
        def _():
            downward(i).wait_send()

    def narrow(r):
        near[pl.ds(r + edge1, TALL), :] = across(m_ref[pl.ds(r, TALL), :], HALF1, True)

    def finish_first(r):
        y = across(mid[pl.ds(r, TALL), :], HALF1, False)
        first_ref[pl.ds(r, TALL), :] = y
        far[pl.ds(r + edge2, TALL), :] = across(y, HALF2, True)

    row_blocks(0, 64, narrow)
    start_up(0)
    row_blocks(rows - 64, 64, narrow)
    start_down(0)

    @pl.when(is_top)
    def _():
        near[0:edge1, :] = jnp.full((edge1, near.shape[1]), jnp.inf, jnp.float32)
        far[0:edge2, :] = jnp.full((edge2, far.shape[1]), jnp.inf, jnp.float32)

    @pl.when(is_bottom)
    def _():
        near[edge1 + rows :, :] = jnp.full((edge1, near.shape[1]), jnp.inf, jnp.float32)
        far[edge2 + rows :, :] = jnp.full((edge2, far.shape[1]), jnp.inf, jnp.float32)

    row_blocks(64, rows - 128, narrow)
    open_rows(near, edge1, rows - 128, mid, 64, HALF1, None, None)
    row_blocks(64, 64, finish_first)
    start_up(1)
    row_blocks(128, rows - 192, finish_first)
    start_down(1)
    receive(0)
    last = range(2, 2 + PIECES)
    open_rows(near, 0, 64, mid, 0, HALF1, is_top, None)
    row_blocks(0, 64, finish_first)
    start_up(*last)
    open_rows(near, rows - 64, 64, mid, rows - 64, HALF1, None, is_bottom)
    row_blocks(rows - 64, 64, finish_first)
    start_down(*last)
    receive(1)
    tiles = width // BC
    for c in range(PIECES):
        receive(2 + c)
        open_rows(far, 0, rows, mid, 0, HALF2, is_top, is_bottom, c * tiles, (c + 1) * tiles)

    def finish_ground(r):
        ground_ref[pl.ds(r, TALL), :] = across(mid[pl.ds(r, TALL), :], HALF2, False)

    row_blocks(0, rows, finish_ground)
    for i in range(2 + PIECES):
        sent(i)


def on_device(n, base_grid, strip_minima, strip_owner, strip_cell):
    held = strip_minima.shape[0]
    capacity = max(2, 2 * held // n)
    rows, cols = base_grid.shape
    vmem = pl.BlockSpec(memory_space=pltpu.VMEM)
    smem = pl.BlockSpec(memory_space=pltpu.SMEM)
    outbox = pl.pallas_call(
        functools.partial(pack_kernel, n, capacity, held),
        out_shape=jax.ShapeDtypeStruct((n, capacity + 1, BR, BC), jnp.float32),
        in_specs=[smem, smem, vmem],
        out_specs=vmem,
        scratch_shapes=[pltpu.SMEM((n,), jnp.int32)],
        compiler_params=pltpu.CompilerParams(vmem_limit_bytes=VMEM_LIMIT),
        name="pack",
    )(strip_owner[:, 0], strip_cell, strip_minima)
    inbox = pl.pallas_call(
        functools.partial(exchange_kernel, n),
        out_shape=jax.ShapeDtypeStruct(outbox.shape, jnp.float32),
        in_specs=[vmem],
        out_specs=vmem,
        scratch_shapes=[
            pltpu.SemaphoreType.DMA((n,)),
            pltpu.SemaphoreType.DMA((n,)),
            pltpu.SemaphoreType.DMA,
        ],
        compiler_params=pltpu.CompilerParams(
            collective_id=1, has_side_effects=True, vmem_limit_bytes=VMEM_LIMIT
        ),
        name="exchange",
    )(outbox)
    tags = inbox[:, capacity, 0, :capacity].astype(jnp.int32).reshape(-1)
    merged = pl.pallas_call(
        functools.partial(merge_kernel, n, capacity, cols // BC),
        out_shape=jax.ShapeDtypeStruct((rows, cols), jnp.float32),
        in_specs=[smem, vmem, vmem],
        out_specs=vmem,
        compiler_params=pltpu.CompilerParams(vmem_limit_bytes=VMEM_LIMIT),
        name="merge",
    )(tags, base_grid, inbox)
    shape = jax.ShapeDtypeStruct((rows, cols), jnp.float32)
    opened_first, ground = pl.pallas_call(
        functools.partial(open_kernel, n),
        out_shape=(shape, shape),
        in_specs=[vmem],
        out_specs=(vmem, vmem),
        scratch_shapes=[
            pltpu.VMEM((rows + 4 * HALF1, cols), jnp.float32),
            pltpu.VMEM((rows + 4 * HALF2, cols), jnp.float32),
            pltpu.VMEM((rows, cols), jnp.float32),
            pltpu.SemaphoreType.DMA((4 + 2 * PIECES,)),
            pltpu.SemaphoreType.DMA((4 + 2 * PIECES,)),
        ],
        compiler_params=pltpu.CompilerParams(
            collective_id=0, has_side_effects=True, vmem_limit_bytes=VMEM_LIMIT
        ),
        name="opening",
    )(merged)
    return (merged, opened_first, ground)


def solution(mesh):
    in_specs = (
        P(("groups", "row"), None),
        P(("groups", "row"), None, None),
        P(("groups", "row"), None),
        P(("groups", "row")),
    )
    out_specs = (P(("groups", "row"), None), P(("groups", "row"), None), P(("groups", "row"), None))
    return jax.shard_map(
        functools.partial(on_device, mesh.shape["row"]),
        mesh=mesh,
        in_specs=in_specs,
        out_specs=out_specs,
        check_vma=False,
    )
```

```python
import functools

import jax
import jax.numpy as jnp
from jax import lax
from jax.experimental import pallas as pl
from jax.experimental.pallas import tpu as pltpu
from jax.sharding import PartitionSpec as P

BR = 8
BC = 128
HALF1 = 32
HALF2 = 64
TALL = 64
PIECES = 4
MESH = pl.DeviceIdType.MESH
VMEM_LIMIT = 48 * 1024 * 1024


def pack_kernel(count, capacity, held, owner_ref, cell_ref, strips_ref, box_ref, used_ref):
    lane = lax.broadcasted_iota(jnp.int32, (1, BC), 1)

    def clear(i, c):
        used_ref[i] = 0
        box_ref[i, capacity] = jnp.full((BR, BC), -1.0, jnp.float32)
        return c

    lax.fori_loop(0, count, clear, 0)

    def place(k, c):
        owner = owner_ref[k]
        slot = used_ref[owner]
        used_ref[owner] = slot + 1
        box_ref[owner, slot] = strips_ref[k]
        tags = box_ref[owner, capacity, 0:1, :]
        box_ref[owner, capacity, 0:1, :] = jnp.where(
            lane == slot, cell_ref[k].astype(jnp.float32), tags
        )
        return c

    lax.fori_loop(0, held, place, 0)


def exchange_kernel(n, box_ref, grid_ref, in_ref, base_ref, send_sem, recv_sem, own_sem, base_sem):
    me = lax.axis_index("row")
    barrier = pltpu.get_barrier_semaphore()

    def greet(k, c):
        peer = lax.rem(me + k, n)
        pl.semaphore_signal(barrier, inc=1, device_id={"row": peer}, device_id_type=MESH)
        return c

    lax.fori_loop(1, n, greet, 0)
    own = pltpu.make_async_copy(box_ref.at[me], in_ref.at[me], own_sem)
    own.start()
    base = pltpu.make_async_copy(grid_ref, base_ref, base_sem)
    base.start()
    pl.semaphore_wait(barrier, n - 1)

    def copy(peer, slot):
        return pltpu.make_async_remote_copy(
            src_ref=box_ref.at[peer],
            dst_ref=in_ref.at[slot],
            send_sem=send_sem.at[peer],
            recv_sem=recv_sem.at[slot],
            device_id={"row": peer},
            device_id_type=MESH,
        )

    def send(k, c):
        copy(lax.rem(me + k, n), me).start()
        return c

    lax.fori_loop(1, n, send, 0)

    def finish(k, c):
        peer = lax.rem(me + k, n)
        copy(peer, peer).wait_recv()
        copy(peer, me).wait_send()
        return c

    lax.fori_loop(1, n, finish, 0)
    own.wait()
    base.wait()


def merge_kernel(n, capacity, col_blocks, tags_ref, base_ref, box_ref, out_ref):
    out_ref[...] = base_ref[...]
    bits = col_blocks.bit_length() - 1

    def place(s, c):
        for j in range(capacity):
            tag = tags_ref[s * capacity + j]
            cell = jnp.maximum(tag, 0)
            row = pl.multiple_of((cell >> bits) * BR, BR)
            col = pl.multiple_of((cell & (col_blocks - 1)) * BC, BC)
            here = (pl.ds(row, BR), pl.ds(col, BC))
            block = jnp.where(tag >= 0, box_ref[s, j], jnp.inf)
            out_ref[here] = jnp.minimum(out_ref[here], block)
        return c

    lax.fori_loop(0, n, place, 0)


def across(x, half, take_min):
    combine = jnp.minimum if take_min else jnp.maximum
    fill = jnp.inf if take_min else -jnp.inf
    cols = x.shape[1]
    run = jnp.concatenate([x, jnp.full((x.shape[0], BC), fill, jnp.float32)], axis=1)
    width = cols + BC
    span = 1
    while span < half:
        run = combine(run, pltpu.roll(run, width - span, axis=1))
        span *= 2
    run = combine(run, pltpu.roll(run, half, axis=1))
    run = combine(run, pltpu.roll(run, width - 1, axis=1))
    return run[:, :cols]


def down(x, half, take_min):
    combine = jnp.minimum if take_min else jnp.maximum
    rows = x.shape[0]
    run = x
    span = 1
    while span < 8:
        run = combine(run, pltpu.roll(run, rows - span, axis=0))
        span *= 2
    while span < 2 * half:
        size = run.shape[0]
        run = combine(run[: size - span], run[span:])
        span *= 2
    keep = rows - 2 * half
    return combine(run[:keep], x[2 * half :])


def open_rows(src, first, out, dst, dst_first, half, is_top, is_bottom, start=0, stop=None):
    def body(c, carry):
        cols = pl.ds(pl.multiple_of(c * BC, BC), BC)
        low = down(src[first : first + out + 4 * half, cols], half, True)
        parts = [low[:half], low[half : half + out], low[half + out :]]
        if is_top is not None:
            parts[0] = jnp.where(is_top, -jnp.inf, parts[0])
        if is_bottom is not None:
            parts[2] = jnp.where(is_bottom, -jnp.inf, parts[2])
        dst[dst_first : dst_first + out, cols] = down(jnp.concatenate(parts, axis=0), half, False)
        return carry

    lax.fori_loop(start, src.shape[1] // BC if stop is None else stop, body, 0)


def row_blocks(first, rows, body):
    def step(i, c):
        body(pl.multiple_of(first + i * TALL, TALL))
        return c

    lax.fori_loop(0, rows // TALL, step, 0)


def open_kernel(n, m_ref, first_ref, ground_ref, near, far, mid, send_sem, recv_sem):
    place = lax.axis_index("row")
    rows = m_ref.shape[0]
    is_top, is_bottom = place == 0, place == n - 1
    edge1, edge2 = 2 * HALF1, 2 * HALF2
    width = m_ref.shape[1] // PIECES

    barrier = pltpu.get_barrier_semaphore()

    @pl.when(place > 0)
    def _():
        pl.semaphore_signal(barrier, inc=1, device_id={"row": place - 1}, device_id_type=MESH)

    @pl.when(place < n - 1)
    def _():
        pl.semaphore_signal(barrier, inc=1, device_id={"row": place + 1}, device_id_type=MESH)

    pl.semaphore_wait(barrier, jnp.where(is_top | is_bottom, 1, 2))

    def move(buf, src, dst, size, cols, peer, at):
        return pltpu.make_async_remote_copy(
            src_ref=buf.at[pl.ds(src, size), cols],
            dst_ref=buf.at[pl.ds(dst, size), cols],
            send_sem=send_sem.at[at],
            recv_sem=recv_sem.at[at],
            device_id={"row": peer},
            device_id_type=MESH,
        )

    plans = [
        (near, (edge1, edge1 + rows, edge1), (rows, 0, edge1), pl.ds(0, m_ref.shape[1])),
        (far, (edge2 + 64, edge2 + rows + 64, 64), (edge2 + 128, 0, 64), pl.ds(0, m_ref.shape[1])),
    ] + [
        (far, (edge2, edge2 + rows, 64), (edge2 + 192, 64, 64), pl.ds(c * width, width))
        for c in range(PIECES)
    ]

    def upward(i):
        return move(plans[i][0], *plans[i][1], plans[i][3], place - 1, 2 * i)

    def downward(i):
        return move(plans[i][0], *plans[i][2], plans[i][3], place + 1, 2 * i + 1)

    def start_up(*which):
        @pl.when(place > 0)
        def _():
            for i in which:
                upward(i).start()

    def start_down(*which):
        @pl.when(place < n - 1)
        def _():
            for i in which:
                downward(i).start()

    def receive(i):
        @pl.when(place < n - 1)
        def _():
            upward(i).wait_recv()

        @pl.when(place > 0)
        def _():
            downward(i).wait_recv()

    def sent(i):
        @pl.when(place > 0)
        def _():
            upward(i).wait_send()

        @pl.when(place < n - 1)
        def _():
            downward(i).wait_send()

    def narrow(r):
        near[pl.ds(r + edge1, TALL), :] = across(m_ref[pl.ds(r, TALL), :], HALF1, True)

    def finish_first(r):
        y = across(mid[pl.ds(r, TALL), :], HALF1, False)
        first_ref[pl.ds(r, TALL), :] = y
        far[pl.ds(r + edge2, TALL), :] = across(y, HALF2, True)

    row_blocks(0, 64, narrow)
    start_up(0)
    row_blocks(rows - 64, 64, narrow)
    start_down(0)

    @pl.when(is_top)
    def _():
        near[0:edge1, :] = jnp.full((edge1, near.shape[1]), jnp.inf, jnp.float32)
        far[0:edge2, :] = jnp.full((edge2, far.shape[1]), jnp.inf, jnp.float32)

    @pl.when(is_bottom)
    def _():
        near[edge1 + rows :, :] = jnp.full((edge1, near.shape[1]), jnp.inf, jnp.float32)
        far[edge2 + rows :, :] = jnp.full((edge2, far.shape[1]), jnp.inf, jnp.float32)

    row_blocks(64, rows - 128, narrow)
    open_rows(near, edge1, rows - 128, mid, 64, HALF1, None, None)
    row_blocks(64, 64, finish_first)
    start_up(1)
    row_blocks(128, rows - 192, finish_first)
    start_down(1)
    receive(0)
    last = range(2, 2 + PIECES)
    open_rows(near, 0, 64, mid, 0, HALF1, is_top, None)
    row_blocks(0, 64, finish_first)
    start_up(*last)
    open_rows(near, rows - 64, 64, mid, rows - 64, HALF1, None, is_bottom)
    row_blocks(rows - 64, 64, finish_first)
    start_down(*last)
    receive(1)
    tiles = width // BC
    cols = m_ref.shape[1]
    for c in range(PIECES):
        receive(2 + c)
        open_rows(far, 0, rows, mid, 0, HALF2, is_top, is_bottom, c * tiles, (c + 1) * tiles)
        lo = max(c * width - BC, 0)
        hi = (c + 1) * width - BC if c < PIECES - 1 else cols
        left, right = max(lo - BC, 0), min(hi + BC, cols)

        def finish_ground(r, lo=lo, hi=hi, left=left, right=right):
            y = across(mid[pl.ds(r, TALL), left:right], HALF2, False)
            ground_ref[pl.ds(r, TALL), lo:hi] = y[:, lo - left : hi - left]

        row_blocks(0, rows, finish_ground)

    for i in range(2 + PIECES):
        sent(i)


def on_device(n, base_grid, strip_minima, strip_owner, strip_cell):
    held = strip_minima.shape[0]
    capacity = max(2, 2 * held // n)
    rows, cols = base_grid.shape
    vmem = pl.BlockSpec(memory_space=pltpu.VMEM)
    smem = pl.BlockSpec(memory_space=pltpu.SMEM)
    outbox = pl.pallas_call(
        functools.partial(pack_kernel, n, capacity, held),
        out_shape=jax.ShapeDtypeStruct((n, capacity + 1, BR, BC), jnp.float32),
        in_specs=[smem, smem, vmem],
        out_specs=vmem,
        scratch_shapes=[pltpu.SMEM((n,), jnp.int32)],
        compiler_params=pltpu.CompilerParams(vmem_limit_bytes=VMEM_LIMIT),
        name="pack",
    )(strip_owner[:, 0], strip_cell, strip_minima)
    inbox, base = pl.pallas_call(
        functools.partial(exchange_kernel, n),
        out_shape=(
            jax.ShapeDtypeStruct(outbox.shape, jnp.float32),
            jax.ShapeDtypeStruct(base_grid.shape, jnp.float32),
        ),
        in_specs=[vmem, pl.BlockSpec(memory_space=pl.ANY)],
        out_specs=(vmem, vmem),
        scratch_shapes=[
            pltpu.SemaphoreType.DMA((n,)),
            pltpu.SemaphoreType.DMA((n,)),
            pltpu.SemaphoreType.DMA,
            pltpu.SemaphoreType.DMA,
        ],
        compiler_params=pltpu.CompilerParams(
            collective_id=1, has_side_effects=True, vmem_limit_bytes=VMEM_LIMIT
        ),
        name="exchange",
    )(outbox, base_grid)
    tags = inbox[:, capacity, 0, :capacity].astype(jnp.int32).reshape(-1)
    merged = pl.pallas_call(
        functools.partial(merge_kernel, n, capacity, cols // BC),
        out_shape=jax.ShapeDtypeStruct((rows, cols), jnp.float32),
        in_specs=[smem, vmem, vmem],
        out_specs=vmem,
        compiler_params=pltpu.CompilerParams(vmem_limit_bytes=VMEM_LIMIT),
        name="merge",
    )(tags, base, inbox)
    shape = jax.ShapeDtypeStruct((rows, cols), jnp.float32)
    opened_first, ground = pl.pallas_call(
        functools.partial(open_kernel, n),
        out_shape=(shape, shape),
        in_specs=[vmem],
        out_specs=(vmem, vmem),
        scratch_shapes=[
            pltpu.VMEM((rows + 4 * HALF1, cols), jnp.float32),
            pltpu.VMEM((rows + 4 * HALF2, cols), jnp.float32),
            pltpu.VMEM((rows, cols), jnp.float32),
            pltpu.SemaphoreType.DMA((4 + 2 * PIECES,)),
            pltpu.SemaphoreType.DMA((4 + 2 * PIECES,)),
        ],
        compiler_params=pltpu.CompilerParams(
            collective_id=0, has_side_effects=True, vmem_limit_bytes=VMEM_LIMIT
        ),
        name="opening",
    )(merged)
    return (merged, opened_first, ground)


def solution(mesh):
    in_specs = (
        P(("groups", "row"), None),
        P(("groups", "row"), None, None),
        P(("groups", "row"), None),
        P(("groups", "row")),
    )
    out_specs = (P(("groups", "row"), None), P(("groups", "row"), None), P(("groups", "row"), None))
    return jax.shard_map(
        functools.partial(on_device, mesh.shape["row"]),
        mesh=mesh,
        in_specs=in_specs,
        out_specs=out_specs,
        check_vma=False,
    )
```

```python
import functools

import jax
import jax.numpy as jnp
from jax import lax
from jax.experimental import pallas as pl
from jax.experimental.pallas import tpu as pltpu
from jax.sharding import PartitionSpec as P

BR = 8
BC = 128
HALF1 = 32
HALF2 = 64
TALL = 64
PIECES = 4
MESH = pl.DeviceIdType.MESH
VMEM_LIMIT = 48 * 1024 * 1024


def pack_kernel(count, capacity, held, owner_ref, cell_ref, strips_ref, box_ref, used_ref):
    lane = lax.broadcasted_iota(jnp.int32, (1, BC), 1)

    def clear(i, c):
        used_ref[i] = 0
        box_ref[i, capacity] = jnp.full((BR, BC), -1.0, jnp.float32)
        return c

    lax.fori_loop(0, count, clear, 0)

    def place(k, c):
        owner = owner_ref[k]
        slot = used_ref[owner]
        used_ref[owner] = slot + 1
        box_ref[owner, slot] = strips_ref[k]
        tags = box_ref[owner, capacity, 0:1, :]
        box_ref[owner, capacity, 0:1, :] = jnp.where(
            lane == slot, cell_ref[k].astype(jnp.float32), tags
        )
        return c

    lax.fori_loop(0, held, place, 0)


def exchange_kernel(n, box_ref, grid_ref, in_ref, base_ref, send_sem, recv_sem, own_sem, base_sem):
    me = lax.axis_index("row")
    barrier = pltpu.get_barrier_semaphore()

    def greet(k, c):
        peer = lax.rem(me + k, n)
        pl.semaphore_signal(barrier, inc=1, device_id={"row": peer}, device_id_type=MESH)
        return c

    lax.fori_loop(1, n, greet, 0)
    own = pltpu.make_async_copy(box_ref.at[me], in_ref.at[me], own_sem)
    own.start()
    base = pltpu.make_async_copy(grid_ref, base_ref, base_sem)
    base.start()
    pl.semaphore_wait(barrier, n - 1)

    def copy(peer, slot):
        return pltpu.make_async_remote_copy(
            src_ref=box_ref.at[peer],
            dst_ref=in_ref.at[slot],
            send_sem=send_sem.at[peer],
            recv_sem=recv_sem.at[slot],
            device_id={"row": peer},
            device_id_type=MESH,
        )

    def send(k, c):
        copy(lax.rem(me + k, n), me).start()
        return c

    lax.fori_loop(1, n, send, 0)

    def finish(k, c):
        peer = lax.rem(me + k, n)
        copy(peer, peer).wait_recv()
        copy(peer, me).wait_send()
        return c

    lax.fori_loop(1, n, finish, 0)
    own.wait()
    base.wait()


def merge_kernel(n, capacity, col_blocks, tags_ref, base_ref, box_ref, out_ref):
    out_ref[...] = base_ref[...]
    bits = col_blocks.bit_length() - 1

    def place(s, c):
        for j in range(capacity):
            tag = tags_ref[s * capacity + j]
            cell = jnp.maximum(tag, 0)
            row = pl.multiple_of((cell >> bits) * BR, BR)
            col = pl.multiple_of((cell & (col_blocks - 1)) * BC, BC)
            here = (pl.ds(row, BR), pl.ds(col, BC))
            block = jnp.where(tag >= 0, box_ref[s, j], jnp.inf)
            out_ref[here] = jnp.minimum(out_ref[here], block)
        return c

    lax.fori_loop(0, n, place, 0)


def across(x, half, take_min):
    combine = jnp.minimum if take_min else jnp.maximum
    fill = jnp.inf if take_min else -jnp.inf
    cols = x.shape[1]
    run = jnp.concatenate([x, jnp.full((x.shape[0], BC), fill, jnp.float32)], axis=1)
    width = cols + BC
    span = 1
    while span < half:
        run = combine(run, pltpu.roll(run, width - span, axis=1))
        span *= 2
    run = combine(run, pltpu.roll(run, half, axis=1))
    run = combine(run, pltpu.roll(run, width - 1, axis=1))
    return run[:, :cols]


def down(x, half, take_min):
    combine = jnp.minimum if take_min else jnp.maximum
    rows = x.shape[0]
    run = x
    span = 1
    while span < 8:
        run = combine(run, pltpu.roll(run, rows - span, axis=0))
        span *= 2
    while span < 2 * half:
        size = run.shape[0]
        run = combine(run[: size - span], run[span:])
        span *= 2
    keep = rows - 2 * half
    return combine(run[:keep], x[2 * half :])


def open_rows(src, first, out, dst, dst_first, half, is_top, is_bottom, start=0, stop=None):
    def body(c, carry):
        cols = pl.ds(pl.multiple_of(c * BC, BC), BC)
        low = down(src[first : first + out + 4 * half, cols], half, True)
        parts = [low[:half], low[half : half + out], low[half + out :]]
        if is_top is not None:
            parts[0] = jnp.where(is_top, -jnp.inf, parts[0])
        if is_bottom is not None:
            parts[2] = jnp.where(is_bottom, -jnp.inf, parts[2])
        dst[dst_first : dst_first + out, cols] = down(jnp.concatenate(parts, axis=0), half, False)
        return carry

    lax.fori_loop(start, src.shape[1] // BC if stop is None else stop, body, 0)


def row_blocks(first, rows, body):
    def step(i, c):
        body(pl.multiple_of(first + i * TALL, TALL))
        return c

    lax.fori_loop(0, rows // TALL, step, 0)


def open_kernel(n, m_ref, first_ref, ground_ref, near, far, mid, send_sem, recv_sem):
    place = lax.axis_index("row")
    rows = m_ref.shape[0]
    is_top, is_bottom = place == 0, place == n - 1
    edge1, edge2 = 2 * HALF1, 2 * HALF2
    width = m_ref.shape[1] // PIECES

    barrier = pltpu.get_barrier_semaphore()

    @pl.when(place > 0)
    def _():
        pl.semaphore_signal(barrier, inc=1, device_id={"row": place - 1}, device_id_type=MESH)

    @pl.when(place < n - 1)
    def _():
        pl.semaphore_signal(barrier, inc=1, device_id={"row": place + 1}, device_id_type=MESH)

    pl.semaphore_wait(barrier, jnp.where(is_top | is_bottom, 1, 2))

    def move(buf, src, dst, size, cols, peer, at):
        return pltpu.make_async_remote_copy(
            src_ref=buf.at[pl.ds(src, size), cols],
            dst_ref=buf.at[pl.ds(dst, size), cols],
            send_sem=send_sem.at[at],
            recv_sem=recv_sem.at[at],
            device_id={"row": peer},
            device_id_type=MESH,
        )

    plans = [
        (near, (edge1, edge1 + rows, edge1), (rows, 0, edge1), pl.ds(0, m_ref.shape[1])),
        (far, (edge2 + 64, edge2 + rows + 64, 64), (edge2 + 128, 0, 64), pl.ds(0, m_ref.shape[1])),
    ] + [
        (far, (edge2, edge2 + rows, 64), (edge2 + 192, 64, 64), pl.ds(c * width, width))
        for c in range(PIECES)
    ]

    def upward(i):
        return move(plans[i][0], *plans[i][1], plans[i][3], place - 1, 2 * i)

    def downward(i):
        return move(plans[i][0], *plans[i][2], plans[i][3], place + 1, 2 * i + 1)

    def start_up(*which):
        @pl.when(place > 0)
        def _():
            for i in which:
                upward(i).start()

    def start_down(*which):
        @pl.when(place < n - 1)
        def _():
            for i in which:
                downward(i).start()

    def receive(i):
        @pl.when(place < n - 1)
        def _():
            upward(i).wait_recv()

        @pl.when(place > 0)
        def _():
            downward(i).wait_recv()

    def sent(i):
        @pl.when(place > 0)
        def _():
            upward(i).wait_send()

        @pl.when(place < n - 1)
        def _():
            downward(i).wait_send()

    def narrow(r):
        near[pl.ds(r + edge1, TALL), :] = across(m_ref[pl.ds(r, TALL), :], HALF1, True)

    def finish_first(r):
        y = across(mid[pl.ds(r, TALL), :], HALF1, False)
        first_ref[pl.ds(r, TALL), :] = y
        far[pl.ds(r + edge2, TALL), :] = across(y, HALF2, True)

    row_blocks(0, 64, narrow)
    start_up(0)
    row_blocks(rows - 64, 64, narrow)
    start_down(0)

    @pl.when(is_top)
    def _():
        near[0:edge1, :] = jnp.full((edge1, near.shape[1]), jnp.inf, jnp.float32)
        far[0:edge2, :] = jnp.full((edge2, far.shape[1]), jnp.inf, jnp.float32)

    @pl.when(is_bottom)
    def _():
        near[edge1 + rows :, :] = jnp.full((edge1, near.shape[1]), jnp.inf, jnp.float32)
        far[edge2 + rows :, :] = jnp.full((edge2, far.shape[1]), jnp.inf, jnp.float32)

    row_blocks(64, rows - 128, narrow)
    open_rows(near, edge1, rows - 128, mid, 64, HALF1, None, None)
    row_blocks(64, 64, finish_first)
    start_up(1)
    row_blocks(128, rows - 192, finish_first)
    start_down(1)
    receive(0)
    last = range(2, 2 + PIECES)
    open_rows(near, 0, 64, mid, 0, HALF1, is_top, None)
    row_blocks(0, 64, finish_first)
    start_up(*last)
    open_rows(near, rows - 64, 64, mid, rows - 64, HALF1, None, is_bottom)
    row_blocks(rows - 64, 64, finish_first)
    start_down(*last)
    receive(1)
    tiles = width // BC
    cols = m_ref.shape[1]
    for c in range(PIECES):
        receive(2 + c)
        open_rows(far, 0, rows, mid, 0, HALF2, is_top, is_bottom, c * tiles, (c + 1) * tiles)
        lo = max(c * width - BC, 0)
        hi = (c + 1) * width - BC if c < PIECES - 1 else cols
        left, right = max(lo - BC, 0), min(hi + BC, cols)

        def finish_ground(i, carry, lo=lo, hi=hi, left=left, right=right):
            here = pl.ds(pl.multiple_of(i * 2 * TALL, 2 * TALL), 2 * TALL)
            y = across(mid[here, left:right], HALF2, False)
            ground_ref[here, lo:hi] = y[:, lo - left : hi - left]
            return carry

        lax.fori_loop(0, rows // (2 * TALL), finish_ground, 0)

    for i in range(2 + PIECES):
        sent(i)


def on_device(n, base_grid, strip_minima, strip_owner, strip_cell):
    held = strip_minima.shape[0]
    capacity = max(2, 2 * held // n)
    rows, cols = base_grid.shape
    vmem = pl.BlockSpec(memory_space=pltpu.VMEM)
    smem = pl.BlockSpec(memory_space=pltpu.SMEM)
    outbox = pl.pallas_call(
        functools.partial(pack_kernel, n, capacity, held),
        out_shape=jax.ShapeDtypeStruct((n, capacity + 1, BR, BC), jnp.float32),
        in_specs=[smem, smem, vmem],
        out_specs=vmem,
        scratch_shapes=[pltpu.SMEM((n,), jnp.int32)],
        compiler_params=pltpu.CompilerParams(vmem_limit_bytes=VMEM_LIMIT),
        name="pack",
    )(strip_owner[:, 0], strip_cell, strip_minima)
    inbox, base = pl.pallas_call(
        functools.partial(exchange_kernel, n),
        out_shape=(
            jax.ShapeDtypeStruct(outbox.shape, jnp.float32),
            jax.ShapeDtypeStruct(base_grid.shape, jnp.float32),
        ),
        in_specs=[vmem, pl.BlockSpec(memory_space=pl.ANY)],
        out_specs=(vmem, vmem),
        scratch_shapes=[
            pltpu.SemaphoreType.DMA((n,)),
            pltpu.SemaphoreType.DMA((n,)),
            pltpu.SemaphoreType.DMA,
            pltpu.SemaphoreType.DMA,
        ],
        compiler_params=pltpu.CompilerParams(
            collective_id=1, has_side_effects=True, vmem_limit_bytes=VMEM_LIMIT
        ),
        name="exchange",
    )(outbox, base_grid)
    tags = inbox[:, capacity, 0, :capacity].astype(jnp.int32).reshape(-1)
    merged = pl.pallas_call(
        functools.partial(merge_kernel, n, capacity, cols // BC),
        out_shape=jax.ShapeDtypeStruct((rows, cols), jnp.float32),
        in_specs=[smem, vmem, vmem],
        out_specs=vmem,
        compiler_params=pltpu.CompilerParams(vmem_limit_bytes=VMEM_LIMIT),
        name="merge",
    )(tags, base, inbox)
    shape = jax.ShapeDtypeStruct((rows, cols), jnp.float32)
    opened_first, ground = pl.pallas_call(
        functools.partial(open_kernel, n),
        out_shape=(shape, shape),
        in_specs=[vmem],
        out_specs=(vmem, vmem),
        scratch_shapes=[
            pltpu.VMEM((rows + 4 * HALF1, cols), jnp.float32),
            pltpu.VMEM((rows + 4 * HALF2, cols), jnp.float32),
            pltpu.VMEM((rows, cols), jnp.float32),
            pltpu.SemaphoreType.DMA((4 + 2 * PIECES,)),
            pltpu.SemaphoreType.DMA((4 + 2 * PIECES,)),
        ],
        compiler_params=pltpu.CompilerParams(
            collective_id=0, has_side_effects=True, vmem_limit_bytes=VMEM_LIMIT
        ),
        name="opening",
    )(merged)
    return (merged, opened_first, ground)


def solution(mesh):
    in_specs = (
        P(("groups", "row"), None),
        P(("groups", "row"), None, None),
        P(("groups", "row"), None),
        P(("groups", "row")),
    )
    out_specs = (P(("groups", "row"), None), P(("groups", "row"), None), P(("groups", "row"), None))
    return jax.shard_map(
        functools.partial(on_device, mesh.shape["row"]),
        mesh=mesh,
        in_specs=in_specs,
        out_specs=out_specs,
        check_vma=False,
    )
```
